256 devices in a mesh: seq: 128 (over x, y, z), head: 2 (over core).
Axes of the slice: x: 4, y: 4, z: 8, core: 2. Of those that a mesh axis runs over, the one named last changes fastest.
Arguments:
- query_tok: bfloat16 [49152, 1536], P('seq', 'head'), may hold values from -110 to 110
- key_tok: bfloat16 [49152, 1536], P('seq', 'head'), may hold values from -5 to 5
- value_tok: bfloat16 [49152, 1536], P('seq', 'head'), may hold values from -6 to 6
- out_weight: bfloat16 [3072, 1536], P(None, 'head'), may hold values from -0.15625 to 0.15625
- grad_out: bfloat16 [49152, 3072], P('seq', 'head'), may hold values from -6 to 6
- tile_pairs: int32 [128, 7], P('seq'), may hold values from -1 to 127, as said below
Outputs:
- mixed_out: bfloat16 [49152, 3072], P('seq', 'head')
- grad_query: bfloat16 [49152, 1536], P('seq', 'head')
- grad_key: bfloat16 [49152, 1536], P('seq', 'head')
- grad_value: bfloat16 [49152, 1536], P('seq', 'head')
The draws below stay inside these ranges and needn't reach their ends.
Inputs may be any that keep to these rules, and one draw needn't show every extreme that they name: `tile_pairs`: slot j of tile g holds g + o_j or -1, with offsets o = (0, 1, -1, 8, -8, 32, -32); slot 0 always holds g; the list is symmetric: b is in the list of g exactly when g is in the list of b.
All inputs are finite; a program needn't handle non-finite values.
Results may differ from the reference program's by a relative error of at most 0.025.
Values may be sent and summed in bfloat16 or wider, within the bound.
No kernel may reach another device: no remote copies, remote signals or barrier semaphores. Data moves between devices by JAX's collectives and lax.ppermute only.
A program may use at most 192 MiB of HBM per device.

```python
import jax
import jax.numpy as jnp
from jax import lax

D = 3072
HEADS = 12
HD = 128
TILE = 384
SLOTS = 7
GW_T = 8
TILES = 128
GH_T = 4
FRAME = 32
TOKENS = 49152


def shared_fields(key):
    query_key = jax.random.fold_in(key, 101)
    key_key = jax.random.fold_in(key, 102)
    shape = (TOKENS, HEADS * HD)
    key_field = jnp.clip(jax.random.normal(key_key, shape, jnp.float32), -4.0, 4.0)
    query_field = jnp.clip(jax.random.normal(query_key, shape, jnp.float32), -4.0, 4.0)
    return (query_field, key_field)


def draw_query_tok(key, part):
    return shared_fields(key)[0].astype(jnp.bfloat16)


def draw_key_tok(key, part):
    return shared_fields(key)[1].astype(jnp.bfloat16)


def draw_tile_pairs(key, part):
    tile_ids = jnp.arange(TILES, dtype=jnp.int32)
    column = tile_ids % GW_T
    tile_row = tile_ids // GW_T % GH_T
    keep_bits = jax.random.randint(jax.random.fold_in(key, 201), (TILES, 3), 0, 4) < 3
    right_pair = keep_bits[:, 0] & (column < GW_T - 1)
    down_pair = keep_bits[:, 2] & (tile_row < GH_T - 1) & (tile_ids + GW_T < TILES)
    later_pair = keep_bits[:, 1] & (tile_ids + FRAME < TILES)
    left_pair = jnp.roll(right_pair, 1) & (column > 0)
    up_pair = jnp.roll(down_pair, GW_T) & (tile_row > 0) & (tile_ids >= GW_T)
    earlier_pair = jnp.roll(later_pair, FRAME) & (tile_ids >= FRAME)
    absent = jnp.full((TILES,), -1, jnp.int32)
    columns = [tile_ids, jnp.where(right_pair, tile_ids + 1, absent), jnp.where(left_pair, tile_ids - 1, absent), jnp.where(down_pair, tile_ids + GW_T, absent), jnp.where(up_pair, tile_ids - GW_T, absent), jnp.where(later_pair, tile_ids + FRAME, absent), jnp.where(earlier_pair, tile_ids - FRAME, absent)]
    return jnp.stack(columns, axis=1).astype(jnp.int32)


def level_of(stream_key, shape, split, smallest, high):
    level, own = 1.0, jax.random.fold_in(stream_key, 6)
    for position, shards_of in split:
        draws = jnp.exp(jax.random.uniform(jax.random.fold_in(own, position), (shards_of,), jnp.float32, smallest / len(split), high / len(split)))
        level = level * jnp.repeat(draws, shape[position] // shards_of).reshape([-1 if axis == position else 1 for axis in range(len(shape))])
    return level


def scatter_about(stream_key, shape, deviation, bound, shards=(), kind=jnp.bfloat16):
    level = level_of(stream_key, shape, shards, -0.22, 0.18) if shards else 1.0
    values = jax.random.normal(stream_key, shape, jnp.float32) * deviation * level
    return jnp.minimum(jnp.maximum(values, -bound), bound).astype(kind)


def setup_inputs(seed: int = 0) -> dict:
    key_of = jax.random.split(jax.random.key(seed), 7)
    query_tok = draw_query_tok(jax.random.fold_in(key_of[6], 71), 0)
    key_tok = draw_key_tok(jax.random.fold_in(key_of[6], 71), 0)
    value_tok = scatter_about(key_of[2], (TOKENS, HEADS * HD), 1.0, 6.0, ((0, 128), (1, 2)))
    out_weight = scatter_about(key_of[3], (D, HEADS * HD), (HEADS * HD) ** -0.5, 0.15625, ((1, 2),))
    grad_out = scatter_about(key_of[4], (TOKENS, D), 1.0, 6.0, ((0, 128), (1, 2)))
    tile_pairs = draw_tile_pairs(jax.random.fold_in(key_of[6], 71), 0)
    return {"query_tok": query_tok, "key_tok": key_tok, "value_tok": value_tok, "out_weight": out_weight, "grad_out": grad_out, "tile_pairs": tile_pairs}


MASKED = -1.0e30


def merge_terms(terms):
    others = terms[1:].astype(jnp.bfloat16).astype(jnp.float32)
    return terms[0] + jnp.sum(others, axis=0)


def reference(query_tok, key_tok, value_tok, out_weight, grad_out, tile_pairs):
    score_scale = HD ** -0.5
    query_tiles = query_tok.reshape(TILES, TILE, HEADS, HD)
    key_tiles = key_tok.reshape(TILES, TILE, HEADS, HD)
    value_tiles = value_tok.reshape(TILES, TILE, HEADS, HD)
    present = tile_pairs >= 0
    safe_index = jnp.maximum(tile_pairs, 0).astype(jnp.int32)
    tile_ids = jnp.arange(TILES, dtype=jnp.int32)

    def forward_tile(tile_id):
        picks = safe_index[tile_id]
        col_mask = jnp.repeat(present[tile_id], TILE)
        queries = query_tiles[tile_id].astype(jnp.float32)
        near_keys = key_tiles[picks].reshape(SLOTS * TILE, HEADS, HD).astype(jnp.float32)
        near_values = value_tiles[picks].reshape(SLOTS * TILE, HEADS, HD).astype(jnp.float32)
        scores = jnp.einsum("qhd,khd->hqk", queries, near_keys) * score_scale
        scores = jnp.where(col_mask[None, None, :], scores, MASKED)
        row_max = jnp.max(scores, axis=-1, keepdims=True)
        log_total = row_max[..., 0] + jnp.log(jnp.sum(jnp.exp(scores - row_max), axis=-1))
        weights = jnp.exp(scores - log_total[..., None]).astype(jnp.bfloat16)
        attended = jnp.einsum("hqk,khd->qhd", weights.astype(jnp.float32), near_values).astype(jnp.bfloat16)
        return attended, log_total

    attended, log_totals = lax.map(forward_tile, tile_ids)
    attended_flat = attended.reshape(TOKENS, HEADS * HD)
    mixed_out = jnp.dot(attended_flat, out_weight.T, preferred_element_type=jnp.float32).astype(jnp.bfloat16)
    grad_attended = jnp.dot(grad_out, out_weight, preferred_element_type=jnp.float32).astype(jnp.bfloat16)
    products = grad_attended.astype(jnp.float32) * attended_flat.astype(jnp.float32)
    row_delta = jnp.sum(products.reshape(TILES, TILE, HEADS, HD), axis=-1).transpose(0, 2, 1)
    grad_tiles = grad_attended.reshape(TILES, TILE, HEADS, HD)

    def query_grads(tile_id):
        picks = safe_index[tile_id]
        col_mask = jnp.repeat(present[tile_id], TILE)
        queries = query_tiles[tile_id].astype(jnp.float32)
        near_keys = key_tiles[picks].reshape(SLOTS * TILE, HEADS, HD).astype(jnp.float32)
        near_values = value_tiles[picks].reshape(SLOTS * TILE, HEADS, HD).astype(jnp.float32)
        scores = jnp.einsum("qhd,khd->hqk", queries, near_keys) * score_scale
        scores = jnp.where(col_mask[None, None, :], scores, MASKED)
        weights = jnp.exp(scores - log_totals[tile_id][..., None])
        own_grads = grad_tiles[tile_id].astype(jnp.float32)
        grad_probs = jnp.einsum("qhd,khd->hqk", own_grads, near_values)
        grad_scores = (weights * (grad_probs - row_delta[tile_id][..., None]) * score_scale).astype(jnp.bfloat16)
        return jnp.einsum("hqk,khd->qhd", grad_scores.astype(jnp.float32), near_keys).astype(jnp.bfloat16)

    def key_grads(tile_id):
        picks = safe_index[tile_id]
        row_mask = jnp.repeat(present[tile_id], TILE)
        near_queries = query_tiles[picks].reshape(SLOTS * TILE, HEADS, HD).astype(jnp.float32)
        near_grads = grad_tiles[picks].reshape(SLOTS * TILE, HEADS, HD).astype(jnp.float32)
        near_lse = log_totals[picks].transpose(1, 0, 2).reshape(HEADS, SLOTS * TILE)
        near_delta = row_delta[picks].transpose(1, 0, 2).reshape(HEADS, SLOTS * TILE)
        own_keys = key_tiles[tile_id].astype(jnp.float32)
        own_values = value_tiles[tile_id].astype(jnp.float32)
        scores = jnp.einsum("qhd,khd->hqk", near_queries, own_keys) * score_scale
        scores = jnp.where(row_mask[None, :, None], scores, MASKED)
        weights = jnp.exp(scores - near_lse[..., None])
        weights_low = weights.astype(jnp.bfloat16).astype(jnp.float32).reshape(HEADS, SLOTS, TILE, TILE)
        grads_slots = near_grads.reshape(SLOTS, TILE, HEADS, HD)
        queries_slots = near_queries.reshape(SLOTS, TILE, HEADS, HD)
        value_terms = jnp.einsum("hsqk,sqhd->skhd", weights_low, grads_slots)
        grad_probs = jnp.einsum("qhd,khd->hqk", near_grads, own_values)
        grad_scores = (weights * (grad_probs - near_delta[..., None]) * score_scale).astype(jnp.bfloat16)
        scores_slots = grad_scores.astype(jnp.float32).reshape(HEADS, SLOTS, TILE, TILE)
        key_terms = jnp.einsum("hsqk,sqhd->skhd", scores_slots, queries_slots)
        return merge_terms(key_terms).astype(jnp.bfloat16), merge_terms(value_terms).astype(jnp.bfloat16)

    grad_query = lax.map(query_grads, tile_ids).reshape(TOKENS, HEADS * HD)
    grad_key, grad_value = lax.map(key_grads, tile_ids)
    return (mixed_out, grad_query, grad_key.reshape(TOKENS, HEADS * HD), grad_value.reshape(TOKENS, HEADS * HD))
```

```python
import functools
import math

import jax
import jax.numpy as jnp
from jax import lax
from jax.experimental import pallas as pl
from jax.experimental.pallas import tpu as pltpu
from jax.sharding import PartitionSpec as P

HD = 128
GW_T = 8
MASKED = -1e30
LOG2E = 1.4426950408889634
VMEM_BYTES = 63 << 20
KV_HEADS = (2, 4)
CALL_HEADS = (1, 1, 2, 1, 1)
TERM_HEADS = (4, 2)
IN_FLIGHT = 5
F32 = jnp.float32
BF16 = jnp.bfloat16
NN = (((1,), (0,)), ((), ()))
NT = (((1,), (1,)), ((), ()))
TN = (((0,), (0,)), ((), ()))
dot = functools.partial(lax.dot_general, preferred_element_type=F32)


def slot_masks(pairs):
    sizes = tile_grid(lax.axis_size("seq"))
    tile, core = lax.axis_index("seq"), lax.axis_index("head")
    place = (tile // (sizes[1] * sizes[2]), tile // sizes[2] % sizes[1], tile % sizes[2])
    slot = {(2, 1): 1, (2, -1): 2, (1, 1): 3, (1, -1): 4, (0, 1): 5, (0, -1): 6}
    here, seam = {}, 0
    for (axis, step), j in slot.items():
        inside = (place[axis] + 1 < sizes[axis]) if step > 0 else (place[axis] > 0)
        listed = (pairs[0, j] >= 0).astype(jnp.int32)
        inside = inside.astype(jnp.int32)
        here[axis, step] = listed * inside
        seam = seam + listed * (1 - inside)
    masks = [(pairs[0, 0] >= 0).astype(jnp.int32)]
    for transfer in STEPS:
        zero, one = [here[axis, -step] for axis, step in transfer]
        masks.append(zero if transfer[0] == transfer[1] else jnp.where(core == 0, zero, one))
    return masks, seam


def attention_kernel(slots, pairs, q, k, v, da, *refs):
    kv = refs[: slots - 1]
    att, dq, own, *terms = refs[-5 - slots : -3]
    s_all, e_all, d_all = refs[-3:]
    rows, width = q.shape
    scale = width**-0.5
    mask, _ = slot_masks(pairs)
    queries, grads = q[...], da[...]
    keys = [k] + [r.at[0] for r in kv]
    values = [v] + [r.at[1] for r in kv]
    outs = [own] + terms
    span = [slice(j * rows, (j + 1) * rows) for j in range(slots)]
    top = None
    for j in range(slots):
        s = dot(queries, keys[j][...], NT)
        s_all[:, span[j]] = s
        part = jnp.maximum(jnp.maximum(s[:, :128], s[:, 128:256]), s[:, 256:])
        part = jnp.where(mask[j] > 0, part, MASKED)
        top = part if top is None else jnp.maximum(top, part)
    row_max = jnp.max(top, axis=1, keepdims=True)
    total, attended = None, None
    for j in range(slots):
        shift = jnp.where(mask[j] > 0, row_max, -MASKED)
        e = jnp.exp2((s_all[:, span[j]] - shift) * (scale * LOG2E))
        part = e[:, :128] + e[:, 128:256] + e[:, 256:]
        total = part if total is None else total + part
        low = e.astype(BF16)
        e_all[:, span[j]] = low
        o = dot(low, values[j][...], NN)
        attended = o if attended is None else attended + o
    inverse = 1.0 / jnp.sum(total, axis=1, keepdims=True)
    attended = (attended * inverse).astype(BF16)
    att[...] = attended
    grads_wide = grads.astype(F32)
    delta = jnp.sum(grads_wide * attended.astype(F32), axis=1, keepdims=True)
    grads_n = (grads_wide * inverse).astype(BF16)
    queries_n = (queries.astype(F32) * (inverse * scale)).astype(BF16)
    grad_query = None
    for j in range(slots):
        dp = dot(grads, values[j][...], NT)
        ds = (e_all[:, span[j]].astype(F32) * (dp - delta)).astype(BF16)
        d_all[:, span[j]] = ds
        g = dot(ds, keys[j][...], NN)
        grad_query = g if grad_query is None else grad_query + g
    dq[...] = (grad_query * (inverse * scale)).astype(BF16)
    for j in range(slots):
        outs[j][0] = dot(d_all[:, span[j]], queries_n, TN).astype(BF16)
        outs[j][1] = dot(e_all[:, span[j]], grads_n, TN).astype(BF16)


def attention_part(first, heads, pairs, q, k, v, da, kvs, kv_first, term_span, done, terms):
    rows, width = q.shape
    term_first, term_heads = term_span
    slots = len(kvs) + 1
    cols = pl.BlockSpec((rows, HD), lambda h: (0, first + h))
    pair_in = pl.BlockSpec((2, rows, HD), lambda h: (0, 0, first - kv_first + h))
    pair_out = pl.BlockSpec((2, rows, HD), lambda h: (0, 0, first - term_first + h))
    whole = jax.ShapeDtypeStruct((rows, width), BF16)
    part = jax.ShapeDtypeStruct((2, rows, term_heads * HD), BF16)
    held = list(done) + list(terms)
    outs = list(range(len(done))) + [2 + i for i in range(len(terms))]
    operands = [pairs, q, k, v, da, *kvs]
    return pl.pallas_call(
        functools.partial(attention_kernel, slots),
        grid=(heads,),
        in_specs=[pl.BlockSpec(memory_space=pltpu.SMEM)]
        + [cols] * 4
        + [pair_in] * len(kvs)
        + [pl.BlockSpec(memory_space=pl.ANY)] * len(held),
        out_specs=[cols] * 2 + [pair_out] * slots,
        out_shape=[whole] * 2 + [part] * slots,
        scratch_shapes=[
            pltpu.VMEM((rows, slots * rows), F32),
            pltpu.VMEM((rows, slots * rows), BF16),
            pltpu.VMEM((rows, slots * rows), BF16),
        ],
        input_output_aliases={len(operands) + i: o for i, o in enumerate(outs)},
        compiler_params=pltpu.CompilerParams(vmem_limit_bytes=VMEM_BYTES),
        cost_estimate=pl.CostEstimate(
            flops=1, bytes_accessed=1, transcendentals=0
        ),
        name=f"attention_{first}",
    )(*operands, *held)


def seam_kernel(pairs, out):
    _, seam = slot_masks(pairs)
    out[...] = jnp.full(out.shape, seam, jnp.int32)


def seam_flag(pairs):
    return pl.pallas_call(
        seam_kernel,
        in_specs=[pl.BlockSpec(memory_space=pltpu.SMEM)],
        out_shape=jax.ShapeDtypeStruct((8, 128), jnp.int32),
        name="seam_flag",
    )(pairs)


def grad_attended_kernel(core, own, other, w_own, w_other, out, acc):
    i = pl.program_id(0)
    part = dot(own[...], w_own[...], NN) + dot(other[...], w_other[...], NN)

    @pl.when(i == 0)
    def _():
        acc[...] = part

    @pl.when(i > 0)
    def _():
        acc[...] += part

    @pl.when(i == pl.num_programs(0) - 1)
    def _():
        out[...] = acc[...].astype(BF16)


def grad_attended_of(core, own, other, weight, block=512):
    rows, depth = own.shape
    width = weight.shape[1]
    steps = depth // block
    spec = pltpu.PrefetchScalarGridSpec(
        num_scalar_prefetch=1,
        grid=(steps,),
        in_specs=[
            pl.BlockSpec((rows, block), lambda i, c: (0, i)),
            pl.BlockSpec((rows, block), lambda i, c: (0, i)),
            pl.BlockSpec((block, width), lambda i, c: (c[0] * steps + i, 0)),
            pl.BlockSpec((block, width), lambda i, c: ((1 - c[0]) * steps + i, 0)),
        ],
        out_specs=pl.BlockSpec((rows, width), lambda i, c: (0, 0)),
        scratch_shapes=[pltpu.VMEM((rows, width), F32)],
    )
    return pl.pallas_call(
        grad_attended_kernel,
        grid_spec=spec,
        out_shape=jax.ShapeDtypeStruct((rows, width), BF16),
        compiler_params=pltpu.CompilerParams(vmem_limit_bytes=VMEM_BYTES),
        cost_estimate=pl.CostEstimate(flops=1, bytes_accessed=1, transcendentals=0),
        name="grad_attended",
    )(core, own, other, weight, weight)


def project_kernel(half, att, w, *refs):
    out = refs[-1]
    part = dot(att[...], w[...], NT)
    if len(refs) > 1:
        part = part + refs[0][...].astype(F32)
    out[...] = part.astype(BF16)


def project(half, att, weight, received=None, block=512):
    rows, width = att.shape
    cols = weight.shape[0] // 2
    steps = cols // block
    tile = pl.BlockSpec((rows, block), lambda i, c: (0, i))
    more = [] if received is None else [received]
    spec = pltpu.PrefetchScalarGridSpec(
        num_scalar_prefetch=1,
        grid=(steps,),
        in_specs=[
            pl.BlockSpec((rows, width), lambda i, c: (0, 0)),
            pl.BlockSpec((block, width), lambda i, c: (c[0] * steps + i, 0)),
        ]
        + [tile] * len(more),
        out_specs=tile,
    )
    return pl.pallas_call(
        project_kernel,
        grid_spec=spec,
        out_shape=jax.ShapeDtypeStruct((rows, cols), BF16),
        compiler_params=pltpu.CompilerParams(vmem_limit_bytes=VMEM_BYTES),
        cost_estimate=pl.CostEstimate(flops=1, bytes_accessed=1, transcendentals=0),
        name="project_sent" if received is None else "project_kept",
    )(half, att, weight, *more)


def add_terms_kernel(*refs):
    parts, (dk, dv) = refs[:7], refs[-2:]
    for i, out in enumerate((dk, dv)):
        total = parts[0][i].astype(F32)
        for part in parts[1:]:
            total = total + part[i].astype(F32)
        out[...] = total.astype(BF16)


def add_terms(first, heads, width, parts, done):
    rows = parts[0].shape[1]
    whole = jax.ShapeDtypeStruct((rows, width), BF16)
    cut = 4
    cols = pl.BlockSpec((rows // cut, heads * HD), lambda i: (i, first // heads))
    pair = pl.BlockSpec((2, rows // cut, heads * HD), lambda i: (0, i, 0))
    return pl.pallas_call(
        add_terms_kernel,
        grid=(cut,),
        in_specs=[pair] * len(parts) + [pl.BlockSpec(memory_space=pl.ANY)] * len(done),
        out_specs=[cols] * 2,
        out_shape=[whole] * 2,
        input_output_aliases={len(parts) + i: i for i in range(len(done))},
        compiler_params=pltpu.CompilerParams(vmem_limit_bytes=VMEM_BYTES),
        cost_estimate=pl.CostEstimate(flops=1, bytes_accessed=1, transcendentals=0),
        name=f"add_terms_{first}",
    )(*parts, *done)


def pack_kernel(k, v, out):
    out[0] = k[...]
    out[1] = v[...]


def pack(first, heads, k, v):
    rows = k.shape[0]
    unit = math.gcd(first, heads)
    source = pl.BlockSpec((rows, unit * HD), lambda i: (0, first // unit + i))
    return pl.pallas_call(
        pack_kernel,
        grid=(heads // unit,),
        in_specs=[source] * 2,
        out_specs=pl.BlockSpec((2, rows, unit * HD), lambda i: (0, 0, i)),
        out_shape=jax.ShapeDtypeStruct((2, rows, heads * HD), BF16),
        compiler_params=pltpu.CompilerParams(vmem_limit_bytes=VMEM_BYTES),
        cost_estimate=pl.CostEstimate(flops=1, bytes_accessed=1, transcendentals=0),
        name=f"pack_{first}",
    )(k, v)


def tile_grid(tiles):
    return (tiles // (4 * GW_T), 4, GW_T)


def moved(tile, sizes, axis, step):
    place = [tile // (sizes[1] * sizes[2]), tile // sizes[2] % sizes[1], tile % sizes[2]]
    place[axis] = (place[axis] + step) % sizes[axis]
    return (place[0] * sizes[1] + place[1]) * sizes[2] + place[2]


STEPS = (
    ((2, 1), (2, -1)),
    ((1, 1), (1, 1)),
    ((1, -1), (1, -1)),
    ((0, 1), (0, 1)),
    ((0, -1), (0, -1)),
    ((2, -1), (2, 1)),
)


def route_of(transfer, sizes, back):
    tiles = sizes[0] * sizes[1] * sizes[2]
    sign = -1 if back else 1
    return [
        (2 * t + core, 2 * moved(t, sizes, axis, sign * step) + core)
        for t in range(tiles)
        for core, (axis, step) in enumerate(transfer)
    ]


def passed_along(block, axis, distance):
    devices = range(lax.axis_size(axis))
    route = [(i - distance, i) for i in devices if i - distance in devices]
    return lax.ppermute(block, axis, route)


def any_lists(query_tok, key_tok, value_tok, out_weight, grad_out, tile_pairs):
    tile_rows, feature_width = query_tok.shape
    head_count = feature_width // HD
    score_scale = HD ** (-0.5)
    tile_count = lax.axis_size("seq")
    frame_tiles = min(4, tile_count // 8) * GW_T
    offsets = (0, 1, -1, GW_T, -GW_T, frame_tiles, -frame_tiles)
    slot_count = len(offsets)
    present = tile_pairs[0] >= 0
    slot_mask = jnp.repeat(present, tile_rows)
    fetched_keys = [key_tok]
    fetched_values = [value_tok]
    for offset in offsets[1:]:
        moved_key, moved_value = passed_along((key_tok, value_tok), "seq", -offset)
        fetched_keys.append(moved_key)
        fetched_values.append(moved_value)
    keys_all = jnp.concatenate(fetched_keys, axis=0).reshape(slot_count * tile_rows, head_count, HD)
    values_all = jnp.concatenate(fetched_values, axis=0).reshape(
        slot_count * tile_rows, head_count, HD
    )
    queries = query_tok.reshape(tile_rows, head_count, HD)
    scores = jnp.einsum("qhd,khd->hqk", queries, keys_all, preferred_element_type=F32) * score_scale
    scores = jnp.where(slot_mask[None, None, :], scores, MASKED)
    row_max = jnp.max(scores, axis=-1, keepdims=True)
    log_total = row_max[..., 0] + jnp.log(jnp.sum(jnp.exp(scores - row_max), axis=-1))
    weights = jnp.exp(scores - log_total[..., None])
    weights_low = weights.astype(BF16)
    attended = jnp.einsum(
        "hqk,khd->qhd", weights_low, values_all, preferred_element_type=F32
    ).astype(BF16)
    attended_flat = attended.reshape(tile_rows, feature_width)
    partial_out = dot(attended_flat, out_weight, NT)
    core, swap = lax.axis_index("head"), [(0, 1), (1, 0)]
    halves = jnp.stack(jnp.split(partial_out, 2, axis=1))
    other_half = lax.ppermute(halves[1 - core].astype(BF16), "head", swap)
    mixed_out = (halves[core] + other_half.astype(F32)).astype(BF16)
    other_grad = lax.ppermute(grad_out, "head", swap)
    grad_full = jnp.where(
        core == 0,
        jnp.concatenate([grad_out, other_grad], axis=1),
        jnp.concatenate([other_grad, grad_out], axis=1),
    )
    grad_attended = dot(grad_full, out_weight, NN).astype(BF16)
    grad_heads = grad_attended.reshape(tile_rows, head_count, HD)
    row_delta = jnp.sum(grad_heads.astype(F32) * attended.astype(F32), axis=-1).T
    grad_probs = jnp.einsum("qhd,khd->hqk", grad_heads, values_all, preferred_element_type=F32)
    grad_scores = (weights * (grad_probs - row_delta[..., None]) * score_scale).astype(BF16)
    grad_query = jnp.einsum("hqk,khd->qhd", grad_scores, keys_all, preferred_element_type=F32)
    grad_query = grad_query.astype(BF16).reshape(tile_rows, feature_width)
    key_terms = jnp.einsum("hqk,qhd->khd", grad_scores, queries, preferred_element_type=F32)
    value_terms = jnp.einsum("hqk,qhd->khd", weights_low, grad_heads, preferred_element_type=F32)
    key_terms = key_terms.reshape(slot_count, tile_rows, feature_width)
    value_terms = value_terms.reshape(slot_count, tile_rows, feature_width)
    grad_key = key_terms[0]
    grad_value = value_terms[0]
    for slot_index in range(1, slot_count):
        sent_key = key_terms[slot_index].astype(BF16)
        sent_value = value_terms[slot_index].astype(BF16)
        back_key, back_value = passed_along((sent_key, sent_value), "seq", offsets[slot_index])
        grad_key = grad_key + back_key.astype(F32)
        grad_value = grad_value + back_value.astype(F32)
    return (mixed_out, grad_query, grad_key.astype(BF16), grad_value.astype(BF16))


def starts_of(heads):
    return [sum(heads[:i]) for i in range(len(heads))]


def group_of(head, heads):
    firsts = starts_of(heads)
    i = max(i for i, f in enumerate(firsts) if f <= head)
    return i, firsts[i], heads[i]


def after(block, *others):
    return lax.optimization_barrier((block, *others))[0]


def on_device(query_tok, key_tok, value_tok, out_weight, grad_out, tile_pairs):
    width = query_tok.shape[1]
    sizes = tile_grid(lax.axis_size("seq"))
    core = lax.axis_index("head")
    core_id = core.astype(jnp.int32)[None]
    sent = []

    def send(block, route):
        if len(sent) >= IN_FLIGHT:
            block = after(block, sent[-IN_FLIGHT])
        sent.append(lax.ppermute(block, ("seq", "head"), route))
        return sent[-1]

    swap = [(2 * t + c, 2 * t + 1 - c) for t in range(lax.axis_size("seq")) for c in (0, 1)]
    routes = [route_of(t, sizes, False) for t in STEPS]
    backs = [route_of(t, sizes, True) for t in STEPS]

    flag = seam_flag(tile_pairs)
    any_seam = lax.pmax(flag[0, 0], "seq")
    other_grad = send(after(grad_out, flag), swap)
    received = []
    for first, heads in zip(starts_of(KV_HEADS), KV_HEADS):
        block = pack(first, heads, key_tok, value_tok)
        if received:
            block = after(block, any_seam, *received[-1])
        received.append([send(block, route) for route in routes])
    grad_attended = grad_attended_of(core_id, grad_out, other_grad, out_weight)

    done, terms, returned, sums = [], [], [], []
    for first, heads in zip(starts_of(CALL_HEADS), CALL_HEADS):
        i, kv_first, _ = group_of(first, KV_HEADS)
        _, term_first, term_heads = group_of(first, TERM_HEADS)
        att, grad_query, *terms = attention_part(
            first,
            heads,
            tile_pairs,
            query_tok,
            key_tok,
            value_tok,
            grad_attended,
            received[i],
            kv_first,
            (term_first, term_heads),
            done,
            terms,
        )
        done = [att, grad_query]
        if first + heads == term_first + term_heads:
            sendable = terms[1:]
            if returned:
                held = returned[-1][1 : 1 + IN_FLIGHT]
                sendable = lax.optimization_barrier((*sendable, *held))[: len(sendable)]
            returned.append([terms[0]] + [send(t, route) for t, route in zip(sendable, backs)])
            terms = []
    partial = project(1 - core_id, att, out_weight)
    other_partial = send(partial, swap)
    for first, heads, parts in zip(starts_of(TERM_HEADS), TERM_HEADS, returned):
        sums = add_terms(first, heads, width, parts, sums)
    mixed_out = project(core_id, att, out_weight, other_partial)

    outs = (mixed_out, grad_query, *sums)
    return lax.cond(
        any_seam > 0,
        lambda outs: any_lists(query_tok, key_tok, value_tok, out_weight, grad_out, tile_pairs),
        lambda outs: outs,
        outs,
    )


def solution(mesh):
    in_specs = (
        P("seq", "head"),
        P("seq", "head"),
        P("seq", "head"),
        P(None, "head"),
        P("seq", "head"),
        P("seq", None),
    )
    out_specs = (P("seq", "head"), P("seq", "head"), P("seq", "head"), P("seq", "head"))
    return jax.shard_map(
        on_device, mesh=mesh, in_specs=in_specs, out_specs=out_specs, check_vma=False
    )
```

```python
import functools

import jax
import jax.numpy as jnp
from jax import lax
from jax.experimental import pallas as pl
from jax.experimental.pallas import tpu as pltpu
from jax.sharding import PartitionSpec as P

HD = 128
GW_T = 8
MASKED = -1e30
LOG2E = 1.4426950408889634
VMEM_BYTES = 63 << 20
KV_HEADS = (6,)
CALL_HEADS = (4, 2)
TERM_HEADS = (4, 2)
IN_FLIGHT = 5
F32 = jnp.float32
BF16 = jnp.bfloat16
NN = (((1,), (0,)), ((), ()))
NT = (((1,), (1,)), ((), ()))
TN = (((0,), (0,)), ((), ()))
dot = functools.partial(lax.dot_general, preferred_element_type=F32)


def slot_masks(pairs):
    sizes = tile_grid(lax.axis_size("seq"))
    tile, core = lax.axis_index("seq"), lax.axis_index("head")
    place = (tile // (sizes[1] * sizes[2]), tile // sizes[2] % sizes[1], tile % sizes[2])
    slot = {(2, 1): 1, (2, -1): 2, (1, 1): 3, (1, -1): 4, (0, 1): 5, (0, -1): 6}
    here, seam = {}, 0
    for (axis, step), j in slot.items():
        inside = (place[axis] + 1 < sizes[axis]) if step > 0 else (place[axis] > 0)
        listed = (pairs[0, j] >= 0).astype(jnp.int32)
        inside = inside.astype(jnp.int32)
        here[axis, step] = listed * inside
        seam = seam + listed * (1 - inside)
    masks = [(pairs[0, 0] >= 0).astype(jnp.int32)]
    for transfer in STEPS:
        zero, one = [here[axis, -step] for axis, step in transfer]
        masks.append(zero if transfer[0] == transfer[1] else jnp.where(core == 0, zero, one))
    return masks, seam


def attention_kernel(slots, pairs, q, k, v, da, *refs):
    kv = refs[: slots - 1]
    att, dq, own, *terms = refs[-5 - slots : -3]
    s_all, e_all, d_all = refs[-3:]
    rows, width = q.shape
    scale = width**-0.5
    mask, _ = slot_masks(pairs)
    queries, grads = q[...], da[...]
    keys = [k] + [r.at[0] for r in kv]
    values = [v] + [r.at[1] for r in kv]
    outs = [own] + terms
    span = [slice(j * rows, (j + 1) * rows) for j in range(slots)]
    top = None
    for j in range(slots):
        s = dot(queries, keys[j][...], NT)
        s_all[:, span[j]] = s
        part = jnp.maximum(jnp.maximum(s[:, :128], s[:, 128:256]), s[:, 256:])
        part = jnp.where(mask[j] > 0, part, MASKED)
        top = part if top is None else jnp.maximum(top, part)
    row_max = jnp.max(top, axis=1, keepdims=True)
    total, attended = None, None
    for j in range(slots):
        shift = jnp.where(mask[j] > 0, row_max, -MASKED)
        e = jnp.exp2((s_all[:, span[j]] - shift) * (scale * LOG2E))
        part = e[:, :128] + e[:, 128:256] + e[:, 256:]
        total = part if total is None else total + part
        low = e.astype(BF16)
        e_all[:, span[j]] = low
        o = dot(low, values[j][...], NN)
        attended = o if attended is None else attended + o
    inverse = 1.0 / jnp.sum(total, axis=1, keepdims=True)
    attended = (attended * inverse).astype(BF16)
    att[...] = attended
    grads_wide = grads.astype(F32)
    delta = jnp.sum(grads_wide * attended.astype(F32), axis=1, keepdims=True)
    grads_n = (grads_wide * inverse).astype(BF16)
    queries_n = (queries.astype(F32) * (inverse * scale)).astype(BF16)
    grad_query = None
    for j in range(slots):
        dp = dot(grads, values[j][...], NT)
        ds = (e_all[:, span[j]].astype(F32) * (dp - delta)).astype(BF16)
        d_all[:, span[j]] = ds
        g = dot(ds, keys[j][...], NN)
        grad_query = g if grad_query is None else grad_query + g
    dq[...] = (grad_query * (inverse * scale)).astype(BF16)
    for j in range(slots):
        outs[j][0] = dot(d_all[:, span[j]], queries_n, TN).astype(BF16)
        outs[j][1] = dot(e_all[:, span[j]], grads_n, TN).astype(BF16)


def attention_part(first, heads, pairs, q, k, v, da, kvs, kv_first, term_span, done, terms):
    rows, width = q.shape
    term_first, term_heads = term_span
    slots = len(kvs) + 1
    cols = pl.BlockSpec((rows, HD), lambda h: (0, first + h))
    pair_in = pl.BlockSpec((2, rows, HD), lambda h: (0, 0, first - kv_first + h))
    pair_out = pl.BlockSpec((2, rows, HD), lambda h: (0, 0, first - term_first + h))
    whole = jax.ShapeDtypeStruct((rows, width), BF16)
    part = jax.ShapeDtypeStruct((2, rows, term_heads * HD), BF16)
    held = list(done) + list(terms)
    outs = list(range(len(done))) + [2 + i for i in range(len(terms))]
    operands = [pairs, q, k, v, da, *kvs]
    return pl.pallas_call(
        functools.partial(attention_kernel, slots),
        grid=(heads,),
        in_specs=[pl.BlockSpec(memory_space=pltpu.SMEM)]
        + [cols] * 4
        + [pair_in] * len(kvs)
        + [pl.BlockSpec(memory_space=pl.ANY)] * len(held),
        out_specs=[cols] * 2 + [pair_out] * slots,
        out_shape=[whole] * 2 + [part] * slots,
        scratch_shapes=[
            pltpu.VMEM((rows, slots * rows), F32),
            pltpu.VMEM((rows, slots * rows), BF16),
            pltpu.VMEM((rows, slots * rows), BF16),
        ],
        input_output_aliases={len(operands) + i: o for i, o in enumerate(outs)},
        compiler_params=pltpu.CompilerParams(vmem_limit_bytes=VMEM_BYTES),
        cost_estimate=pl.CostEstimate(
            flops=1, bytes_accessed=1, transcendentals=0
        ),
        name=f"attention_{first}",
    )(*operands, *held)


def seam_kernel(pairs, out):
    _, seam = slot_masks(pairs)
    out[0, 0] = seam


def seam_flag(pairs):
    return pl.pallas_call(
        seam_kernel,
        in_specs=[pl.BlockSpec(memory_space=pltpu.SMEM)],
        out_specs=pl.BlockSpec(memory_space=pltpu.SMEM),
        out_shape=jax.ShapeDtypeStruct((1, 1), jnp.int32),
        name="seam_flag",
    )(pairs)


def grad_attended_kernel(core, own, other, w_own, w_other, out, acc):
    i = pl.program_id(0)
    part = dot(own[...], w_own[...], NN) + dot(other[...], w_other[...], NN)

    @pl.when(i == 0)
    def _():
        acc[...] = part

    @pl.when(i > 0)
    def _():
        acc[...] += part

    @pl.when(i == pl.num_programs(0) - 1)
    def _():
        out[...] = acc[...].astype(BF16)


def grad_attended_of(core, own, other, weight, block=768):
    rows, depth = own.shape
    width = weight.shape[1]
    steps = depth // block
    spec = pltpu.PrefetchScalarGridSpec(
        num_scalar_prefetch=1,
        grid=(steps,),
        in_specs=[
            pl.BlockSpec((rows, block), lambda i, c: (0, i)),
            pl.BlockSpec((rows, block), lambda i, c: (0, i)),
            pl.BlockSpec((block, width), lambda i, c: (c[0] * steps + i, 0)),
            pl.BlockSpec((block, width), lambda i, c: ((1 - c[0]) * steps + i, 0)),
        ],
        out_specs=pl.BlockSpec((rows, width), lambda i, c: (0, 0)),
        scratch_shapes=[pltpu.VMEM((rows, width), F32)],
    )
    return pl.pallas_call(
        grad_attended_kernel,
        grid_spec=spec,
        out_shape=jax.ShapeDtypeStruct((rows, width), BF16),
        compiler_params=pltpu.CompilerParams(vmem_limit_bytes=VMEM_BYTES),
        cost_estimate=pl.CostEstimate(flops=1, bytes_accessed=1, transcendentals=0),
        name="grad_attended",
    )(core, own, other, weight, weight)


def project_kernel(half, att, w, *refs):
    out = refs[-1]
    part = dot(att[...], w[...], NT)
    if len(refs) > 1:
        part = part + refs[0][...].astype(F32)
    out[...] = part.astype(BF16)


def project(half, att, weight, received=None, block=768):
    rows, width = att.shape
    cols = weight.shape[0] // 2
    steps = cols // block
    tile = pl.BlockSpec((rows, block), lambda i, c: (0, i))
    more = [] if received is None else [received]
    spec = pltpu.PrefetchScalarGridSpec(
        num_scalar_prefetch=1,
        grid=(steps,),
        in_specs=[
            pl.BlockSpec((rows, width), lambda i, c: (0, 0)),
            pl.BlockSpec((block, width), lambda i, c: (c[0] * steps + i, 0)),
        ]
        + [tile] * len(more),
        out_specs=tile,
    )
    return pl.pallas_call(
        project_kernel,
        grid_spec=spec,
        out_shape=jax.ShapeDtypeStruct((rows, cols), BF16),
        compiler_params=pltpu.CompilerParams(vmem_limit_bytes=VMEM_BYTES),
        cost_estimate=pl.CostEstimate(flops=1, bytes_accessed=1, transcendentals=0),
        name="project_sent" if received is None else "project_kept",
    )(half, att, weight, *more)


def add_terms_kernel(*refs):
    parts, (dk, dv) = refs[:7], refs[-2:]
    for i, out in enumerate((dk, dv)):
        total = parts[0][i].astype(F32)
        for part in parts[1:]:
            total = total + part[i].astype(F32)
        out[...] = total.astype(BF16)


def add_terms(first, heads, width, parts, done):
    rows = parts[0].shape[1]
    whole = jax.ShapeDtypeStruct((rows, width), BF16)
    cut = 2
    cols = pl.BlockSpec((rows // cut, heads * HD), lambda i: (i, first // heads))
    pair = pl.BlockSpec((2, rows // cut, heads * HD), lambda i: (0, i, 0))
    return pl.pallas_call(
        add_terms_kernel,
        grid=(cut,),
        in_specs=[pair] * len(parts) + [pl.BlockSpec(memory_space=pl.ANY)] * len(done),
        out_specs=[cols] * 2,
        out_shape=[whole] * 2,
        input_output_aliases={len(parts) + i: i for i in range(len(done))},
        compiler_params=pltpu.CompilerParams(vmem_limit_bytes=VMEM_BYTES),
        cost_estimate=pl.CostEstimate(flops=1, bytes_accessed=1, transcendentals=0),
        name=f"add_terms_{first}",
    )(*parts, *done)


def pack_kernel(k, v, out):
    out[0] = k[...]
    out[1] = v[...]


def pack(first, heads, k, v, cut=2):
    rows = k.shape[0]
    wide = heads * HD
    source = pl.BlockSpec((rows // cut, wide), lambda i: (i, first // heads))
    return pl.pallas_call(
        pack_kernel,
        grid=(cut,),
        in_specs=[source] * 2,
        out_specs=pl.BlockSpec((2, rows // cut, wide), lambda i: (0, i, 0)),
        out_shape=jax.ShapeDtypeStruct((2, rows, wide), BF16),
        compiler_params=pltpu.CompilerParams(vmem_limit_bytes=VMEM_BYTES),
        cost_estimate=pl.CostEstimate(flops=1, bytes_accessed=1, transcendentals=0),
        name=f"pack_{first}",
    )(k, v)


def tile_grid(tiles):
    return (tiles // (4 * GW_T), 4, GW_T)


def moved(tile, sizes, axis, step):
    place = [tile // (sizes[1] * sizes[2]), tile // sizes[2] % sizes[1], tile % sizes[2]]
    place[axis] = (place[axis] + step) % sizes[axis]
    return (place[0] * sizes[1] + place[1]) * sizes[2] + place[2]


STEPS = (
    ((2, 1), (2, -1)),
    ((1, 1), (1, 1)),
    ((1, -1), (1, -1)),
    ((0, 1), (0, 1)),
    ((0, -1), (0, -1)),
    ((2, -1), (2, 1)),
)


def route_of(transfer, sizes, back):
    tiles = sizes[0] * sizes[1] * sizes[2]
    sign = -1 if back else 1
    return [
        (2 * t + core, 2 * moved(t, sizes, axis, sign * step) + core)
        for t in range(tiles)
        for core, (axis, step) in enumerate(transfer)
    ]


def passed_along(block, axis, distance):
    devices = range(lax.axis_size(axis))
    route = [(i - distance, i) for i in devices if i - distance in devices]
    return lax.ppermute(block, axis, route)


def any_lists(query_tok, key_tok, value_tok, out_weight, grad_out, tile_pairs):
    tile_rows, feature_width = query_tok.shape
    head_count = feature_width // HD
    score_scale = HD ** (-0.5)
    tile_count = lax.axis_size("seq")
    frame_tiles = min(4, tile_count // 8) * GW_T
    offsets = (0, 1, -1, GW_T, -GW_T, frame_tiles, -frame_tiles)
    slot_count = len(offsets)
    present = tile_pairs[0] >= 0
    slot_mask = jnp.repeat(present, tile_rows)
    fetched_keys = [key_tok]
    fetched_values = [value_tok]
    for offset in offsets[1:]:
        moved_key, moved_value = passed_along((key_tok, value_tok), "seq", -offset)
        fetched_keys.append(moved_key)
        fetched_values.append(moved_value)
    keys_all = jnp.concatenate(fetched_keys, axis=0).reshape(slot_count * tile_rows, head_count, HD)
    values_all = jnp.concatenate(fetched_values, axis=0).reshape(
        slot_count * tile_rows, head_count, HD
    )
    queries = query_tok.reshape(tile_rows, head_count, HD)
    scores = jnp.einsum("qhd,khd->hqk", queries, keys_all, preferred_element_type=F32) * score_scale
    scores = jnp.where(slot_mask[None, None, :], scores, MASKED)
    row_max = jnp.max(scores, axis=-1, keepdims=True)
    log_total = row_max[..., 0] + jnp.log(jnp.sum(jnp.exp(scores - row_max), axis=-1))
    weights = jnp.exp(scores - log_total[..., None])
    weights_low = weights.astype(BF16)
    attended = jnp.einsum(
        "hqk,khd->qhd", weights_low, values_all, preferred_element_type=F32
    ).astype(BF16)
    attended_flat = attended.reshape(tile_rows, feature_width)
    partial_out = dot(attended_flat, out_weight, NT)
    core, swap = lax.axis_index("head"), [(0, 1), (1, 0)]
    halves = jnp.stack(jnp.split(partial_out, 2, axis=1))
    other_half = lax.ppermute(halves[1 - core].astype(BF16), "head", swap)
    mixed_out = (halves[core] + other_half.astype(F32)).astype(BF16)
    other_grad = lax.ppermute(grad_out, "head", swap)
    grad_full = jnp.where(
        core == 0,
        jnp.concatenate([grad_out, other_grad], axis=1),
        jnp.concatenate([other_grad, grad_out], axis=1),
    )
    grad_attended = dot(grad_full, out_weight, NN).astype(BF16)
    grad_heads = grad_attended.reshape(tile_rows, head_count, HD)
    row_delta = jnp.sum(grad_heads.astype(F32) * attended.astype(F32), axis=-1).T
    grad_probs = jnp.einsum("qhd,khd->hqk", grad_heads, values_all, preferred_element_type=F32)
    grad_scores = (weights * (grad_probs - row_delta[..., None]) * score_scale).astype(BF16)
    grad_query = jnp.einsum("hqk,khd->qhd", grad_scores, keys_all, preferred_element_type=F32)
    grad_query = grad_query.astype(BF16).reshape(tile_rows, feature_width)
    key_terms = jnp.einsum("hqk,qhd->khd", grad_scores, queries, preferred_element_type=F32)
    value_terms = jnp.einsum("hqk,qhd->khd", weights_low, grad_heads, preferred_element_type=F32)
    key_terms = key_terms.reshape(slot_count, tile_rows, feature_width)
    value_terms = value_terms.reshape(slot_count, tile_rows, feature_width)
    grad_key = key_terms[0]
    grad_value = value_terms[0]
    for slot_index in range(1, slot_count):
        sent_key = key_terms[slot_index].astype(BF16)
        sent_value = value_terms[slot_index].astype(BF16)
        back_key, back_value = passed_along((sent_key, sent_value), "seq", offsets[slot_index])
        grad_key = grad_key + back_key.astype(F32)
        grad_value = grad_value + back_value.astype(F32)
    return (mixed_out, grad_query, grad_key.astype(BF16), grad_value.astype(BF16))


def starts_of(heads):
    return [sum(heads[:i]) for i in range(len(heads))]


def group_of(head, heads):
    firsts = starts_of(heads)
    i = max(i for i, f in enumerate(firsts) if f <= head)
    return i, firsts[i], heads[i]


def after(block, *others):
    return lax.optimization_barrier((block, *others))[0]


def on_device(query_tok, key_tok, value_tok, out_weight, grad_out, tile_pairs):
    width = query_tok.shape[1]
    sizes = tile_grid(lax.axis_size("seq"))
    core = lax.axis_index("head")
    core_id = core.astype(jnp.int32)[None]
    sent = []

    def send(block, route):
        if len(sent) >= IN_FLIGHT:
            block = after(block, sent[-IN_FLIGHT])
        sent.append(lax.ppermute(block, ("seq", "head"), route))
        return sent[-1]

    swap = [(2 * t + c, 2 * t + 1 - c) for t in range(lax.axis_size("seq")) for c in (0, 1)]
    routes = [route_of(t, sizes, False) for t in STEPS]
    backs = [route_of(t, sizes, True) for t in STEPS]

    flag = seam_flag(tile_pairs)
    other_grad = lax.ppermute(after(grad_out, flag), ("seq", "head"), swap)
    received = []
    for first, heads in zip(starts_of(KV_HEADS), KV_HEADS):
        block = pack(first, heads, key_tok, value_tok)
        if received:
            block = after(block, *received[-1])
        received.append([send(block, route) for route in routes[:-1]])
    grad_attended = grad_attended_of(core_id, grad_out, other_grad, out_weight)
    received[0].append(send(after(block, grad_attended), routes[-1]))
    flag = after(flag.reshape(()), grad_attended, received[0][0])
    any_seam = lax.pmax(flag, "seq")
    tile_pairs = after(tile_pairs, any_seam)

    done, terms, returned, sums = [], [], [], []
    for first, heads in zip(starts_of(CALL_HEADS), CALL_HEADS):
        i, kv_first, _ = group_of(first, KV_HEADS)
        _, term_first, term_heads = group_of(first, TERM_HEADS)
        att, grad_query, *terms = attention_part(
            first,
            heads,
            tile_pairs,
            query_tok,
            key_tok,
            value_tok,
            grad_attended,
            received[i],
            kv_first,
            (term_first, term_heads),
            done,
            terms,
        )
        done = [att, grad_query]
        if first + heads == term_first + term_heads:
            sendable = terms[1:]
            if returned:
                last, *sendable = lax.optimization_barrier((waiting, *sendable, *returned[-1][1:]))
                sent.clear()
                sendable = sendable[: len(terms) - 1]
                returned[-1].append(send(last, backs[-1]))
            *early, waiting = sendable
            returned.append([terms[0]] + [send(t, route) for t, route in zip(early, backs)])
            terms = []
    returned[-1].append(send(waiting, backs[-1]))
    partial = project(1 - core_id, att, out_weight)
    other_partial = lax.ppermute(partial, ("seq", "head"), swap)
    for first, heads, parts in zip(starts_of(TERM_HEADS), TERM_HEADS, returned):
        sums = add_terms(first, heads, width, parts, sums)
    mixed_out = project(core_id, att, out_weight, other_partial)

    outs = (mixed_out, grad_query, *sums)
    return lax.cond(
        any_seam > 0,
        lambda outs: any_lists(query_tok, key_tok, value_tok, out_weight, grad_out, tile_pairs),
        lambda outs: outs,
        outs,
    )


def solution(mesh):
    in_specs = (
        P("seq", "head"),
        P("seq", "head"),
        P("seq", "head"),
        P(None, "head"),
        P("seq", "head"),
        P("seq", None),
    )
    out_specs = (P("seq", "head"), P("seq", "head"), P("seq", "head"), P("seq", "head"))
    return jax.shard_map(
        on_device, mesh=mesh, in_specs=in_specs, out_specs=out_specs, check_vma=False
    )
```

```python
import functools

import jax
import jax.numpy as jnp
from jax import lax
from jax.experimental import pallas as pl
from jax.experimental.pallas import tpu as pltpu
from jax.sharding import PartitionSpec as P

HD = 128
GW_T = 8
MASKED = -1e30
LOG2E = 1.4426950408889634
VMEM_BYTES = 63 << 20
KV_HEADS = (6,)
CALL_HEADS = (4, 2)
TERM_HEADS = (4, 2)
IN_FLIGHT = 5
F32 = jnp.float32
BF16 = jnp.bfloat16
NN = (((1,), (0,)), ((), ()))
NT = (((1,), (1,)), ((), ()))
TN = (((0,), (0,)), ((), ()))
dot = functools.partial(lax.dot_general, preferred_element_type=F32)


def slot_masks(pairs):
    sizes = tile_grid(lax.axis_size("seq"))
    tile, core = lax.axis_index("seq"), lax.axis_index("head")
    place = (tile // (sizes[1] * sizes[2]), tile // sizes[2] % sizes[1], tile % sizes[2])
    slot = {(2, 1): 1, (2, -1): 2, (1, 1): 3, (1, -1): 4, (0, 1): 5, (0, -1): 6}
    here, seam = {}, 0
    for (axis, step), j in slot.items():
        inside = (place[axis] + 1 < sizes[axis]) if step > 0 else (place[axis] > 0)
        listed = (pairs[0, j] >= 0).astype(jnp.int32)
        inside = inside.astype(jnp.int32)
        here[axis, step] = listed * inside
        seam = seam + listed * (1 - inside)
    masks = [(pairs[0, 0] >= 0).astype(jnp.int32)]
    for transfer in STEPS:
        zero, one = [here[axis, -step] for axis, step in transfer]
        masks.append(zero if transfer[0] == transfer[1] else jnp.where(core == 0, zero, one))
    return masks, seam


def attention_kernel(slots, pairs, q, k, v, da, *refs):
    kv = refs[: slots - 1]
    att, dq, own, *terms = refs[-5 - slots : -3]
    s_all, e_all, d_all = refs[-3:]
    rows, width = q.shape
    scale = width**-0.5
    mask, _ = slot_masks(pairs)
    queries, grads = q[...], da[...]
    keys = [k] + [r.at[0] for r in kv]
    values = [v] + [r.at[1] for r in kv]
    outs = [own] + terms
    span = [slice(j * rows, (j + 1) * rows) for j in range(slots)]
    top = None
    for j in range(slots):
        s = dot(queries, keys[j][...], NT)
        s_all[:, span[j]] = s
        part = jnp.maximum(jnp.maximum(s[:, :128], s[:, 128:256]), s[:, 256:])
        part = jnp.where(mask[j] > 0, part, MASKED)
        top = part if top is None else jnp.maximum(top, part)
    row_max = jnp.max(top, axis=1, keepdims=True)
    total, attended = None, None
    for j in range(slots):
        shift = jnp.where(mask[j] > 0, row_max, -MASKED)
        e = jnp.exp2((s_all[:, span[j]] - shift) * (scale * LOG2E))
        part = e[:, :128] + e[:, 128:256] + e[:, 256:]
        total = part if total is None else total + part
        low = e.astype(BF16)
        e_all[:, span[j]] = low
        o = dot(low, values[j][...], NN)
        attended = o if attended is None else attended + o
    inverse = 1.0 / jnp.sum(total, axis=1, keepdims=True)
    attended = (attended * inverse).astype(BF16)
    att[...] = attended
    grads_wide = grads.astype(F32)
    delta = jnp.sum(grads_wide * attended.astype(F32), axis=1, keepdims=True)
    grads_n = (grads_wide * inverse).astype(BF16)
    queries_n = (queries.astype(F32) * (inverse * scale)).astype(BF16)
    grad_query = None
    for j in range(slots):
        dp = dot(grads, values[j][...], NT)
        ds = (e_all[:, span[j]].astype(F32) * (dp - delta)).astype(BF16)
        d_all[:, span[j]] = ds
        g = dot(ds, keys[j][...], NN)
        grad_query = g if grad_query is None else grad_query + g
    dq[...] = (grad_query * (inverse * scale)).astype(BF16)
    for j in range(slots):
        outs[j][0] = dot(d_all[:, span[j]], queries_n, TN).astype(BF16)
        outs[j][1] = dot(e_all[:, span[j]], grads_n, TN).astype(BF16)


def attention_part(first, heads, pairs, q, k, v, da, kvs, kv_first, term_span, done, terms):
    rows, width = q.shape
    term_first, term_heads = term_span
    slots = len(kvs) + 1
    cols = pl.BlockSpec((rows, HD), lambda h: (0, first + h))
    pair_in = pl.BlockSpec((2, rows, HD), lambda h: (0, 0, first - kv_first + h))
    pair_out = pl.BlockSpec((2, rows, HD), lambda h: (0, 0, first - term_first + h))
    whole = jax.ShapeDtypeStruct((rows, width), BF16)
    part = jax.ShapeDtypeStruct((2, rows, term_heads * HD), BF16)
    held = list(done) + list(terms)
    outs = list(range(len(done))) + [2 + i for i in range(len(terms))]
    operands = [pairs, q, k, v, da, *kvs]
    return pl.pallas_call(
        functools.partial(attention_kernel, slots),
        grid=(heads,),
        in_specs=[pl.BlockSpec(memory_space=pltpu.SMEM)]
        + [cols] * 4
        + [pair_in] * len(kvs)
        + [pl.BlockSpec(memory_space=pl.ANY)] * len(held),
        out_specs=[cols] * 2 + [pair_out] * slots,
        out_shape=[whole] * 2 + [part] * slots,
        scratch_shapes=[
            pltpu.VMEM((rows, slots * rows), F32),
            pltpu.VMEM((rows, slots * rows), BF16),
            pltpu.VMEM((rows, slots * rows), BF16),
        ],
        input_output_aliases={len(operands) + i: o for i, o in enumerate(outs)},
        compiler_params=pltpu.CompilerParams(vmem_limit_bytes=VMEM_BYTES),
        cost_estimate=pl.CostEstimate(
            flops=1, bytes_accessed=1, transcendentals=0
        ),
        name=f"attention_{first}",
    )(*operands, *held)


def seam_kernel(pairs, out):
    _, seam = slot_masks(pairs)
    out[0, 0] = seam


def seam_flag(pairs):
    return pl.pallas_call(
        seam_kernel,
        in_specs=[pl.BlockSpec(memory_space=pltpu.SMEM)],
        out_specs=pl.BlockSpec(memory_space=pltpu.SMEM),
        out_shape=jax.ShapeDtypeStruct((1, 1), jnp.int32),
        name="seam_flag",
    )(pairs)


def grad_attended_kernel(core, own, other, w_own, w_other, out, acc):
    i = pl.program_id(0)
    part = dot(own[...], w_own[...], NN) + dot(other[...], w_other[...], NN)

    @pl.when(i == 0)
    def _():
        acc[...] = part

    @pl.when(i > 0)
    def _():
        acc[...] += part

    @pl.when(i == pl.num_programs(0) - 1)
    def _():
        out[...] = acc[...].astype(BF16)


def grad_attended_of(core, own, other, weight, block=768):
    rows, depth = own.shape
    width = weight.shape[1]
    steps = depth // block
    spec = pltpu.PrefetchScalarGridSpec(
        num_scalar_prefetch=1,
        grid=(steps,),
        in_specs=[
            pl.BlockSpec((rows, block), lambda i, c: (0, i)),
            pl.BlockSpec((rows, block), lambda i, c: (0, i)),
            pl.BlockSpec((block, width), lambda i, c: (c[0] * steps + i, 0)),
            pl.BlockSpec((block, width), lambda i, c: ((1 - c[0]) * steps + i, 0)),
        ],
        out_specs=pl.BlockSpec((rows, width), lambda i, c: (0, 0)),
        scratch_shapes=[pltpu.VMEM((rows, width), F32)],
    )
    return pl.pallas_call(
        grad_attended_kernel,
        grid_spec=spec,
        out_shape=jax.ShapeDtypeStruct((rows, width), BF16),
        compiler_params=pltpu.CompilerParams(vmem_limit_bytes=VMEM_BYTES),
        cost_estimate=pl.CostEstimate(flops=1, bytes_accessed=1, transcendentals=0),
        name="grad_attended",
    )(core, own, other, weight, weight)


def project_kernel(half, att, w, *refs):
    out = refs[-1]
    part = dot(att[...], w[...], NT)
    if len(refs) > 1:
        part = part + refs[0][...].astype(F32)
    out[...] = part.astype(BF16)


def project(half, att, weight, received=None, block=768):
    rows, width = att.shape
    cols = weight.shape[0] // 2
    steps = cols // block
    tile = pl.BlockSpec((rows, block), lambda i, c: (0, i))
    more = [] if received is None else [received]
    spec = pltpu.PrefetchScalarGridSpec(
        num_scalar_prefetch=1,
        grid=(steps,),
        in_specs=[
            pl.BlockSpec((rows, width), lambda i, c: (0, 0)),
            pl.BlockSpec((block, width), lambda i, c: (c[0] * steps + i, 0)),
        ]
        + [tile] * len(more),
        out_specs=tile,
    )
    return pl.pallas_call(
        project_kernel,
        grid_spec=spec,
        out_shape=jax.ShapeDtypeStruct((rows, cols), BF16),
        compiler_params=pltpu.CompilerParams(vmem_limit_bytes=VMEM_BYTES),
        cost_estimate=pl.CostEstimate(flops=1, bytes_accessed=1, transcendentals=0),
        name="project_sent" if received is None else "project_kept",
    )(half, att, weight, *more)


def add_terms_kernel(*refs):
    parts, (dk, dv) = refs[:7], refs[-2:]
    for i, out in enumerate((dk, dv)):
        total = parts[0][i].astype(F32)
        for part in parts[1:]:
            total = total + part[i].astype(F32)
        out[...] = total.astype(BF16)


def add_terms(first, heads, width, parts, done):
    rows = parts[0].shape[1]
    whole = jax.ShapeDtypeStruct((rows, width), BF16)
    cut = 2
    cols = pl.BlockSpec((rows // cut, heads * HD), lambda i: (i, first // heads))
    pair = pl.BlockSpec((2, rows // cut, heads * HD), lambda i: (0, i, 0))
    return pl.pallas_call(
        add_terms_kernel,
        grid=(cut,),
        in_specs=[pair] * len(parts) + [pl.BlockSpec(memory_space=pl.ANY)] * len(done),
        out_specs=[cols] * 2,
        out_shape=[whole] * 2,
        input_output_aliases={len(parts) + i: i for i in range(len(done))},
        compiler_params=pltpu.CompilerParams(vmem_limit_bytes=VMEM_BYTES),
        cost_estimate=pl.CostEstimate(flops=1, bytes_accessed=1, transcendentals=0),
        name=f"add_terms_{first}",
    )(*parts, *done)


def pack_kernel(k, v, out):
    out[0] = k[...]
    out[1] = v[...]


def pack(first, heads, k, v, cut=2):
    rows = k.shape[0]
    wide = heads * HD
    source = pl.BlockSpec((rows // cut, wide), lambda i: (i, first // heads))
    return pl.pallas_call(
        pack_kernel,
        grid=(cut,),
        in_specs=[source] * 2,
        out_specs=pl.BlockSpec((2, rows // cut, wide), lambda i: (0, i, 0)),
        out_shape=jax.ShapeDtypeStruct((2, rows, wide), BF16),
        compiler_params=pltpu.CompilerParams(vmem_limit_bytes=VMEM_BYTES),
        cost_estimate=pl.CostEstimate(flops=1, bytes_accessed=1, transcendentals=0),
        name=f"pack_{first}",
    )(k, v)


def tile_grid(tiles):
    return (tiles // (4 * GW_T), 4, GW_T)


def moved(tile, sizes, axis, step):
    place = [tile // (sizes[1] * sizes[2]), tile // sizes[2] % sizes[1], tile % sizes[2]]
    place[axis] = (place[axis] + step) % sizes[axis]
    return (place[0] * sizes[1] + place[1]) * sizes[2] + place[2]


STEPS = (
    ((2, 1), (2, -1)),
    ((1, 1), (1, 1)),
    ((1, -1), (1, -1)),
    ((0, 1), (0, 1)),
    ((0, -1), (0, -1)),
    ((2, -1), (2, 1)),
)


def route_of(transfer, sizes, back):
    tiles = sizes[0] * sizes[1] * sizes[2]
    sign = -1 if back else 1
    return [
        (2 * t + core, 2 * moved(t, sizes, axis, sign * step) + core)
        for t in range(tiles)
        for core, (axis, step) in enumerate(transfer)
    ]


def passed_along(block, axis, distance):
    devices = range(lax.axis_size(axis))
    route = [(i - distance, i) for i in devices if i - distance in devices]
    return lax.ppermute(block, axis, route)


def any_lists(query_tok, key_tok, value_tok, out_weight, grad_out, tile_pairs):
    tile_rows, feature_width = query_tok.shape
    head_count = feature_width // HD
    score_scale = HD ** (-0.5)
    tile_count = lax.axis_size("seq")
    frame_tiles = min(4, tile_count // 8) * GW_T
    offsets = (0, 1, -1, GW_T, -GW_T, frame_tiles, -frame_tiles)
    slot_count = len(offsets)
    present = tile_pairs[0] >= 0
    slot_mask = jnp.repeat(present, tile_rows)
    fetched_keys = [key_tok]
    fetched_values = [value_tok]
    for offset in offsets[1:]:
        moved_key, moved_value = passed_along((key_tok, value_tok), "seq", -offset)
        fetched_keys.append(moved_key)
        fetched_values.append(moved_value)
    keys_all = jnp.concatenate(fetched_keys, axis=0).reshape(slot_count * tile_rows, head_count, HD)
    values_all = jnp.concatenate(fetched_values, axis=0).reshape(
        slot_count * tile_rows, head_count, HD
    )
    queries = query_tok.reshape(tile_rows, head_count, HD)
    scores = jnp.einsum("qhd,khd->hqk", queries, keys_all, preferred_element_type=F32) * score_scale
    scores = jnp.where(slot_mask[None, None, :], scores, MASKED)
    row_max = jnp.max(scores, axis=-1, keepdims=True)
    log_total = row_max[..., 0] + jnp.log(jnp.sum(jnp.exp(scores - row_max), axis=-1))
    weights = jnp.exp(scores - log_total[..., None])
    weights_low = weights.astype(BF16)
    attended = jnp.einsum(
        "hqk,khd->qhd", weights_low, values_all, preferred_element_type=F32
    ).astype(BF16)
    attended_flat = attended.reshape(tile_rows, feature_width)
    partial_out = dot(attended_flat, out_weight, NT)
    core, swap = lax.axis_index("head"), [(0, 1), (1, 0)]
    halves = jnp.stack(jnp.split(partial_out, 2, axis=1))
    other_half = lax.ppermute(halves[1 - core].astype(BF16), "head", swap)
    mixed_out = (halves[core] + other_half.astype(F32)).astype(BF16)
    other_grad = lax.ppermute(grad_out, "head", swap)
    grad_full = jnp.where(
        core == 0,
        jnp.concatenate([grad_out, other_grad], axis=1),
        jnp.concatenate([other_grad, grad_out], axis=1),
    )
    grad_attended = dot(grad_full, out_weight, NN).astype(BF16)
    grad_heads = grad_attended.reshape(tile_rows, head_count, HD)
    row_delta = jnp.sum(grad_heads.astype(F32) * attended.astype(F32), axis=-1).T
    grad_probs = jnp.einsum("qhd,khd->hqk", grad_heads, values_all, preferred_element_type=F32)
    grad_scores = (weights * (grad_probs - row_delta[..., None]) * score_scale).astype(BF16)
    grad_query = jnp.einsum("hqk,khd->qhd", grad_scores, keys_all, preferred_element_type=F32)
    grad_query = grad_query.astype(BF16).reshape(tile_rows, feature_width)
    key_terms = jnp.einsum("hqk,qhd->khd", grad_scores, queries, preferred_element_type=F32)
    value_terms = jnp.einsum("hqk,qhd->khd", weights_low, grad_heads, preferred_element_type=F32)
    key_terms = key_terms.reshape(slot_count, tile_rows, feature_width)
    value_terms = value_terms.reshape(slot_count, tile_rows, feature_width)
    grad_key = key_terms[0]
    grad_value = value_terms[0]
    for slot_index in range(1, slot_count):
        sent_key = key_terms[slot_index].astype(BF16)
        sent_value = value_terms[slot_index].astype(BF16)
        back_key, back_value = passed_along((sent_key, sent_value), "seq", offsets[slot_index])
        grad_key = grad_key + back_key.astype(F32)
        grad_value = grad_value + back_value.astype(F32)
    return (mixed_out, grad_query, grad_key.astype(BF16), grad_value.astype(BF16))


def starts_of(heads):
    return [sum(heads[:i]) for i in range(len(heads))]


def group_of(head, heads):
    firsts = starts_of(heads)
    i = max(i for i, f in enumerate(firsts) if f <= head)
    return i, firsts[i], heads[i]


def after(block, *others):
    return lax.optimization_barrier((block, *others))[0]


def on_device(query_tok, key_tok, value_tok, out_weight, grad_out, tile_pairs):
    width = query_tok.shape[1]
    sizes = tile_grid(lax.axis_size("seq"))
    core = lax.axis_index("head")
    core_id = core.astype(jnp.int32)[None]
    sent = []

    def send(block, route):
        if len(sent) >= IN_FLIGHT:
            block = after(block, sent[-IN_FLIGHT])
        sent.append(lax.ppermute(block, ("seq", "head"), route))
        return sent[-1]

    swap = [(2 * t + c, 2 * t + 1 - c) for t in range(lax.axis_size("seq")) for c in (0, 1)]
    routes = [route_of(t, sizes, False) for t in STEPS]
    backs = [route_of(t, sizes, True) for t in STEPS]

    flag = seam_flag(tile_pairs)
    other_grad = lax.ppermute(after(grad_out, flag), ("seq", "head"), swap)
    received = []
    for first, heads in zip(starts_of(KV_HEADS), KV_HEADS):
        block = pack(first, heads, key_tok, value_tok)
        if received:
            block = after(block, *received[-1])
        received.append([send(block, route) for route in routes[:-1]])
    grad_attended = grad_attended_of(core_id, grad_out, other_grad, out_weight)
    received[0].append(send(after(block, grad_attended), routes[-1]))
    flag = after(flag.reshape(()), grad_attended, received[0][0])
    any_seam = lax.pmax(flag, "seq")
    tile_pairs = after(tile_pairs, any_seam)

    done, terms, returned, sums = [], [], [], []
    for first, heads in zip(starts_of(CALL_HEADS), CALL_HEADS):
        i, kv_first, _ = group_of(first, KV_HEADS)
        _, term_first, term_heads = group_of(first, TERM_HEADS)
        att, grad_query, *terms = attention_part(
            first,
            heads,
            tile_pairs,
            query_tok,
            key_tok,
            value_tok,
            grad_attended,
            received[i],
            kv_first,
            (term_first, term_heads),
            done,
            terms,
        )
        done = [att, grad_query]
        if first + heads == term_first + term_heads:
            if not returned:
                *early, waiting = terms[1:]
                returned.append([terms[0]] + [send(t, route) for t, route in zip(early, backs)])
                terms = []
    partial = project(1 - core_id, att, out_weight)
    other_partial = lax.ppermute(partial, ("seq", "head"), swap)
    waiting, *parts = lax.optimization_barrier((waiting, *terms[1:], *returned[0][1:]))
    parts = parts[:6]

    def give(i, block):
        return lax.ppermute(block, ("seq", "head"), backs[i])

    returned[0].append(give(5, waiting))
    got = {i: give(i, parts[i]) for i in (1, 2, 3)}
    got[4] = give(4, after(parts[4], other_partial))
    mixed_out = project(core_id, att, out_weight, other_partial)
    got[0] = give(0, after(parts[0], got[1], mixed_out))
    got[5] = give(5, after(parts[5], got[2], mixed_out))
    returned.append([terms[0]] + [got[i] for i in range(6)])
    for first, heads, parts in zip(starts_of(TERM_HEADS), TERM_HEADS, returned):
        sums = add_terms(first, heads, width, parts, sums)

    outs = (mixed_out, grad_query, *sums)
    return lax.cond(
        any_seam > 0,
        lambda outs: any_lists(query_tok, key_tok, value_tok, out_weight, grad_out, tile_pairs),
        lambda outs: outs,
        outs,
    )


def solution(mesh):
    in_specs = (
        P("seq", "head"),
        P("seq", "head"),
        P("seq", "head"),
        P(None, "head"),
        P("seq", "head"),
        P("seq", None),
    )
    out_specs = (P("seq", "head"), P("seq", "head"), P("seq", "head"), P("seq", "head"))
    return jax.shard_map(
        on_device, mesh=mesh, in_specs=in_specs, out_specs=out_specs, check_vma=False
    )
```

```python
import functools

import jax
import jax.numpy as jnp
from jax import lax
from jax.experimental import pallas as pl
from jax.experimental.pallas import tpu as pltpu
from jax.sharding import PartitionSpec as P

HD = 128
GW_T = 8
MASKED = -1e30
LOG2E = 1.4426950408889634
VMEM_BYTES = 63 << 20
KV_HEADS = (6,)
CALL_HEADS = (4, 2)
TERM_HEADS = (4, 2)
IN_FLIGHT = 5
F32 = jnp.float32
BF16 = jnp.bfloat16
NN = (((1,), (0,)), ((), ()))
NT = (((1,), (1,)), ((), ()))
TN = (((0,), (0,)), ((), ()))
dot = functools.partial(lax.dot_general, preferred_element_type=F32)


def slot_masks(pairs):
    sizes = tile_grid(lax.axis_size("seq"))
    tile, core = lax.axis_index("seq"), lax.axis_index("head")
    place = (tile // (sizes[1] * sizes[2]), tile // sizes[2] % sizes[1], tile % sizes[2])
    slot = {(2, 1): 1, (2, -1): 2, (1, 1): 3, (1, -1): 4, (0, 1): 5, (0, -1): 6}
    here, seam = {}, 0
    for (axis, step), j in slot.items():
        inside = (place[axis] + 1 < sizes[axis]) if step > 0 else (place[axis] > 0)
        listed = (pairs[0, j] >= 0).astype(jnp.int32)
        inside = inside.astype(jnp.int32)
        here[axis, step] = listed * inside
        seam = seam + listed * (1 - inside)
    masks = [(pairs[0, 0] >= 0).astype(jnp.int32)]
    for transfer in STEPS:
        zero, one = [here[axis, -step] for axis, step in transfer]
        masks.append(zero if transfer[0] == transfer[1] else jnp.where(core == 0, zero, one))
    return masks, seam


def attention_kernel(slots, pairs, q, k, v, da, *refs):
    kv = refs[: slots - 1]
    att, dq, own, *terms = refs[-5 - slots : -3]
    s_all, e_all, d_all = refs[-3:]
    rows, width = q.shape
    scale = width**-0.5
    mask, _ = slot_masks(pairs)
    queries, grads = q[...], da[...]
    keys = [k] + [r.at[0] for r in kv]
    values = [v] + [r.at[1] for r in kv]
    outs = [own] + terms
    span = [slice(j * rows, (j + 1) * rows) for j in range(slots)]
    top = None
    for j in range(slots):
        s = dot(queries, keys[j][...], NT)
        s_all[:, span[j]] = s
        part = jnp.maximum(jnp.maximum(s[:, :128], s[:, 128:256]), s[:, 256:])
        part = jnp.where(mask[j] > 0, part, MASKED)
        top = part if top is None else jnp.maximum(top, part)
    row_max = jnp.max(top, axis=1, keepdims=True)
    total, attended = None, None
    for j in range(slots):
        shift = jnp.where(mask[j] > 0, row_max, -MASKED)
        e = jnp.exp2((s_all[:, span[j]] - shift) * (scale * LOG2E))
        part = e[:, :128] + e[:, 128:256] + e[:, 256:]
        total = part if total is None else total + part
        low = e.astype(BF16)
        e_all[:, span[j]] = low
        o = dot(low, values[j][...], NN)
        attended = o if attended is None else attended + o
    inverse = 1.0 / jnp.sum(total, axis=1, keepdims=True)
    attended = (attended * inverse).astype(BF16)
    att[...] = attended
    grads_wide = grads.astype(F32)
    delta = jnp.sum(grads_wide * attended.astype(F32), axis=1, keepdims=True)
    grads_n = (grads_wide * inverse).astype(BF16)
    queries_n = (queries.astype(F32) * (inverse * scale)).astype(BF16)
    grad_query = None
    for j in range(slots):
        dp = dot(grads, values[j][...], NT)
        ds = (e_all[:, span[j]].astype(F32) * (dp - delta)).astype(BF16)
        d_all[:, span[j]] = ds
        g = dot(ds, keys[j][...], NN)
        grad_query = g if grad_query is None else grad_query + g
    dq[...] = (grad_query * (inverse * scale)).astype(BF16)
    for j in range(slots):
        outs[j][0] = dot(d_all[:, span[j]], queries_n, TN).astype(BF16)
        outs[j][1] = dot(e_all[:, span[j]], grads_n, TN).astype(BF16)


def attention_part(first, heads, pairs, q, k, v, da, kvs, kv_first, term_span, done, terms):
    rows, width = q.shape
    term_first, term_heads = term_span
    slots = len(kvs) + 1
    cols = pl.BlockSpec((rows, HD), lambda h: (0, first + h))
    pair_in = pl.BlockSpec((2, rows, HD), lambda h: (0, 0, first - kv_first + h))
    pair_out = pl.BlockSpec((2, rows, HD), lambda h: (0, 0, first - term_first + h))
    whole = jax.ShapeDtypeStruct((rows, width), BF16)
    part = jax.ShapeDtypeStruct((2, rows, term_heads * HD), BF16)
    held = list(done) + list(terms)
    outs = list(range(len(done))) + [2 + i for i in range(len(terms))]
    operands = [pairs, q, k, v, da, *kvs]
    return pl.pallas_call(
        functools.partial(attention_kernel, slots),
        grid=(heads,),
        in_specs=[pl.BlockSpec(memory_space=pltpu.SMEM)]
        + [cols] * 4
        + [pair_in] * len(kvs)
        + [pl.BlockSpec(memory_space=pl.ANY)] * len(held),
        out_specs=[cols] * 2 + [pair_out] * slots,
        out_shape=[whole] * 2 + [part] * slots,
        scratch_shapes=[
            pltpu.VMEM((rows, slots * rows), F32),
            pltpu.VMEM((rows, slots * rows), BF16),
            pltpu.VMEM((rows, slots * rows), BF16),
        ],
        input_output_aliases={len(operands) + i: o for i, o in enumerate(outs)},
        compiler_params=pltpu.CompilerParams(vmem_limit_bytes=VMEM_BYTES),
        cost_estimate=pl.CostEstimate(
            flops=1, bytes_accessed=1, transcendentals=0
        ),
        name=f"attention_{first}",
    )(*operands, *held)


def seam_kernel(pairs, out):
    _, seam = slot_masks(pairs)
    out[0, 0] = seam


def seam_flag(pairs):
    return pl.pallas_call(
        seam_kernel,
        in_specs=[pl.BlockSpec(memory_space=pltpu.SMEM)],
        out_specs=pl.BlockSpec(memory_space=pltpu.SMEM),
        out_shape=jax.ShapeDtypeStruct((1, 1), jnp.int32),
        name="seam_flag",
    )(pairs)


def grad_attended_kernel(core, own, other, w_own, w_other, out, acc):
    i = pl.program_id(0)
    part = dot(own[...], w_own[...], NN) + dot(other[...], w_other[...], NN)

    @pl.when(i == 0)
    def _():
        acc[...] = part

    @pl.when(i > 0)
    def _():
        acc[...] += part

    @pl.when(i == pl.num_programs(0) - 1)
    def _():
        out[...] = acc[...].astype(BF16)


def grad_attended_of(core, own, other, weight, block=768):
    rows, depth = own.shape
    width = weight.shape[1]
    steps = depth // block
    spec = pltpu.PrefetchScalarGridSpec(
        num_scalar_prefetch=1,
        grid=(steps,),
        in_specs=[
            pl.BlockSpec((rows, block), lambda i, c: (0, i)),
            pl.BlockSpec((rows, block), lambda i, c: (0, i)),
            pl.BlockSpec((block, width), lambda i, c: (c[0] * steps + i, 0)),
            pl.BlockSpec((block, width), lambda i, c: ((1 - c[0]) * steps + i, 0)),
        ],
        out_specs=pl.BlockSpec((rows, width), lambda i, c: (0, 0)),
        scratch_shapes=[pltpu.VMEM((rows, width), F32)],
    )
    return pl.pallas_call(
        grad_attended_kernel,
        grid_spec=spec,
        out_shape=jax.ShapeDtypeStruct((rows, width), BF16),
        compiler_params=pltpu.CompilerParams(vmem_limit_bytes=VMEM_BYTES),
        cost_estimate=pl.CostEstimate(flops=1, bytes_accessed=1, transcendentals=0),
        name="grad_attended",
    )(core, own, other, weight, weight)


def project_kernel(half, att, w, *refs):
    out = refs[-1]
    part = dot(att[...], w[...], NT)
    if len(refs) > 1:
        part = part + refs[0][...].astype(F32)
    out[...] = part.astype(BF16)


def project(half, att, weight, received=None, block=1536):
    rows, width = att.shape
    cols = weight.shape[0] // 2
    steps = cols // block
    tile = pl.BlockSpec((rows, block), lambda i, c: (0, i))
    more = [] if received is None else [received]
    spec = pltpu.PrefetchScalarGridSpec(
        num_scalar_prefetch=1,
        grid=(steps,),
        in_specs=[
            pl.BlockSpec((rows, width), lambda i, c: (0, 0)),
            pl.BlockSpec((block, width), lambda i, c: (c[0] * steps + i, 0)),
        ]
        + [tile] * len(more),
        out_specs=tile,
    )
    return pl.pallas_call(
        project_kernel,
        grid_spec=spec,
        out_shape=jax.ShapeDtypeStruct((rows, cols), BF16),
        compiler_params=pltpu.CompilerParams(vmem_limit_bytes=VMEM_BYTES),
        cost_estimate=pl.CostEstimate(flops=1, bytes_accessed=1, transcendentals=0),
        name="project_sent" if received is None else "project_kept",
    )(half, att, weight, *more)


def add_terms_kernel(*refs):
    parts, (dk, dv) = refs[:7], refs[-2:]
    for i, out in enumerate((dk, dv)):
        total = parts[0][i].astype(F32)
        for part in parts[1:]:
            total = total + part[i].astype(F32)
        out[...] = total.astype(BF16)


def add_terms(first, heads, width, parts, done):
    rows = parts[0].shape[1]
    whole = jax.ShapeDtypeStruct((rows, width), BF16)
    cut = 2
    cols = pl.BlockSpec((rows // cut, heads * HD), lambda i: (i, first // heads))
    pair = pl.BlockSpec((2, rows // cut, heads * HD), lambda i: (0, i, 0))
    return pl.pallas_call(
        add_terms_kernel,
        grid=(cut,),
        in_specs=[pair] * len(parts) + [pl.BlockSpec(memory_space=pl.ANY)] * len(done),
        out_specs=[cols] * 2,
        out_shape=[whole] * 2,
        input_output_aliases={len(parts) + i: i for i in range(len(done))},
        compiler_params=pltpu.CompilerParams(vmem_limit_bytes=VMEM_BYTES),
        cost_estimate=pl.CostEstimate(flops=1, bytes_accessed=1, transcendentals=0),
        name=f"add_terms_{first}",
    )(*parts, *done)


def pack_kernel(k, v, out):
    out[0] = k[...]
    out[1] = v[...]


def pack(first, heads, k, v, cut=2):
    rows = k.shape[0]
    wide = heads * HD
    source = pl.BlockSpec((rows // cut, wide), lambda i: (i, first // heads))
    return pl.pallas_call(
        pack_kernel,
        grid=(cut,),
        in_specs=[source] * 2,
        out_specs=pl.BlockSpec((2, rows // cut, wide), lambda i: (0, i, 0)),
        out_shape=jax.ShapeDtypeStruct((2, rows, wide), BF16),
        compiler_params=pltpu.CompilerParams(vmem_limit_bytes=VMEM_BYTES),
        cost_estimate=pl.CostEstimate(flops=1, bytes_accessed=1, transcendentals=0),
        name=f"pack_{first}",
    )(k, v)


def tile_grid(tiles):
    return (tiles // (4 * GW_T), 4, GW_T)


def moved(tile, sizes, axis, step):
    place = [tile // (sizes[1] * sizes[2]), tile // sizes[2] % sizes[1], tile % sizes[2]]
    place[axis] = (place[axis] + step) % sizes[axis]
    return (place[0] * sizes[1] + place[1]) * sizes[2] + place[2]


STEPS = (
    ((2, 1), (2, -1)),
    ((1, 1), (1, 1)),
    ((1, -1), (1, -1)),
    ((0, 1), (0, 1)),
    ((0, -1), (0, -1)),
    ((2, -1), (2, 1)),
)


def route_of(transfer, sizes, back):
    tiles = sizes[0] * sizes[1] * sizes[2]
    sign = -1 if back else 1
    return [
        (2 * t + core, 2 * moved(t, sizes, axis, sign * step) + core)
        for t in range(tiles)
        for core, (axis, step) in enumerate(transfer)
    ]


def passed_along(block, axis, distance):
    devices = range(lax.axis_size(axis))
    route = [(i - distance, i) for i in devices if i - distance in devices]
    return lax.ppermute(block, axis, route)


def any_lists(query_tok, key_tok, value_tok, out_weight, grad_out, tile_pairs):
    tile_rows, feature_width = query_tok.shape
    head_count = feature_width // HD
    score_scale = HD ** (-0.5)
    tile_count = lax.axis_size("seq")
    frame_tiles = min(4, tile_count // 8) * GW_T
    offsets = (0, 1, -1, GW_T, -GW_T, frame_tiles, -frame_tiles)
    slot_count = len(offsets)
    present = tile_pairs[0] >= 0
    slot_mask = jnp.repeat(present, tile_rows)
    fetched_keys = [key_tok]
    fetched_values = [value_tok]
    for offset in offsets[1:]:
        moved_key, moved_value = passed_along((key_tok, value_tok), "seq", -offset)
        fetched_keys.append(moved_key)
        fetched_values.append(moved_value)
    keys_all = jnp.concatenate(fetched_keys, axis=0).reshape(slot_count * tile_rows, head_count, HD)
    values_all = jnp.concatenate(fetched_values, axis=0).reshape(
        slot_count * tile_rows, head_count, HD
    )
    queries = query_tok.reshape(tile_rows, head_count, HD)
    scores = jnp.einsum("qhd,khd->hqk", queries, keys_all, preferred_element_type=F32) * score_scale
    scores = jnp.where(slot_mask[None, None, :], scores, MASKED)
    row_max = jnp.max(scores, axis=-1, keepdims=True)
    log_total = row_max[..., 0] + jnp.log(jnp.sum(jnp.exp(scores - row_max), axis=-1))
    weights = jnp.exp(scores - log_total[..., None])
    weights_low = weights.astype(BF16)
    attended = jnp.einsum(
        "hqk,khd->qhd", weights_low, values_all, preferred_element_type=F32
    ).astype(BF16)
    attended_flat = attended.reshape(tile_rows, feature_width)
    partial_out = dot(attended_flat, out_weight, NT)
    core, swap = lax.axis_index("head"), [(0, 1), (1, 0)]
    halves = jnp.stack(jnp.split(partial_out, 2, axis=1))
    other_half = lax.ppermute(halves[1 - core].astype(BF16), "head", swap)
    mixed_out = (halves[core] + other_half.astype(F32)).astype(BF16)
    other_grad = lax.ppermute(grad_out, "head", swap)
    grad_full = jnp.where(
        core == 0,
        jnp.concatenate([grad_out, other_grad], axis=1),
        jnp.concatenate([other_grad, grad_out], axis=1),
    )
    grad_attended = dot(grad_full, out_weight, NN).astype(BF16)
    grad_heads = grad_attended.reshape(tile_rows, head_count, HD)
    row_delta = jnp.sum(grad_heads.astype(F32) * attended.astype(F32), axis=-1).T
    grad_probs = jnp.einsum("qhd,khd->hqk", grad_heads, values_all, preferred_element_type=F32)
    grad_scores = (weights * (grad_probs - row_delta[..., None]) * score_scale).astype(BF16)
    grad_query = jnp.einsum("hqk,khd->qhd", grad_scores, keys_all, preferred_element_type=F32)
    grad_query = grad_query.astype(BF16).reshape(tile_rows, feature_width)
    key_terms = jnp.einsum("hqk,qhd->khd", grad_scores, queries, preferred_element_type=F32)
    value_terms = jnp.einsum("hqk,qhd->khd", weights_low, grad_heads, preferred_element_type=F32)
    key_terms = key_terms.reshape(slot_count, tile_rows, feature_width)
    value_terms = value_terms.reshape(slot_count, tile_rows, feature_width)
    grad_key = key_terms[0]
    grad_value = value_terms[0]
    for slot_index in range(1, slot_count):
        sent_key = key_terms[slot_index].astype(BF16)
        sent_value = value_terms[slot_index].astype(BF16)
        back_key, back_value = passed_along((sent_key, sent_value), "seq", offsets[slot_index])
        grad_key = grad_key + back_key.astype(F32)
        grad_value = grad_value + back_value.astype(F32)
    return (mixed_out, grad_query, grad_key.astype(BF16), grad_value.astype(BF16))


def starts_of(heads):
    return [sum(heads[:i]) for i in range(len(heads))]


def group_of(head, heads):
    firsts = starts_of(heads)
    i = max(i for i, f in enumerate(firsts) if f <= head)
    return i, firsts[i], heads[i]


def after(block, *others):
    return lax.optimization_barrier((block, *others))[0]


def on_device(query_tok, key_tok, value_tok, out_weight, grad_out, tile_pairs):
    width = query_tok.shape[1]
    sizes = tile_grid(lax.axis_size("seq"))
    core = lax.axis_index("head")
    core_id = core.astype(jnp.int32)[None]
    sent = []

    def send(block, route):
        if len(sent) >= IN_FLIGHT:
            block = after(block, sent[-IN_FLIGHT])
        sent.append(lax.ppermute(block, ("seq", "head"), route))
        return sent[-1]

    swap = [(2 * t + c, 2 * t + 1 - c) for t in range(lax.axis_size("seq")) for c in (0, 1)]
    routes = [route_of(t, sizes, False) for t in STEPS]
    backs = [route_of(t, sizes, True) for t in STEPS]

    flag = seam_flag(tile_pairs)
    other_grad = lax.ppermute(after(grad_out, flag), ("seq", "head"), swap)
    received = []
    for first, heads in zip(starts_of(KV_HEADS), KV_HEADS):
        block = pack(first, heads, key_tok, value_tok)
        if received:
            block = after(block, *received[-1])
        received.append([send(block, route) for route in routes[:-1]])
    grad_attended = grad_attended_of(core_id, grad_out, other_grad, out_weight)
    received[0].append(send(after(block, grad_attended), routes[-1]))
    flag = after(flag.reshape(()), grad_attended, received[0][0])
    any_seam = lax.pmax(flag, "seq")
    tile_pairs = after(tile_pairs, any_seam)

    done, terms, returned, sums = [], [], [], []
    for first, heads in zip(starts_of(CALL_HEADS), CALL_HEADS):
        i, kv_first, _ = group_of(first, KV_HEADS)
        _, term_first, term_heads = group_of(first, TERM_HEADS)
        att, grad_query, *terms = attention_part(
            first,
            heads,
            tile_pairs,
            query_tok,
            key_tok,
            value_tok,
            grad_attended,
            received[i],
            kv_first,
            (term_first, term_heads),
            done,
            terms,
        )
        done = [att, grad_query]
        if first + heads == term_first + term_heads:
            if not returned:
                *early, waiting = terms[1:]
                returned.append([terms[0]] + [send(t, route) for t, route in zip(early, backs)])
                terms = []
    partial = project(1 - core_id, att, out_weight)
    other_partial = lax.ppermute(partial, ("seq", "head"), swap)
    waiting, *parts = lax.optimization_barrier((waiting, *terms[1:], *returned[0][1:]))
    parts = parts[:6]

    def give(i, block):
        return lax.ppermute(block, ("seq", "head"), backs[i])

    returned[0].append(give(5, waiting))
    got = {i: give(i, parts[i]) for i in (1, 2, 3)}
    got[4] = give(4, after(parts[4], other_partial))
    mixed_out = project(core_id, att, out_weight, other_partial)
    got[0] = give(0, after(parts[0], got[1], mixed_out))
    got[5] = give(5, after(parts[5], got[2], mixed_out))
    returned.append([terms[0]] + [got[i] for i in range(6)])
    for first, heads, parts in zip(starts_of(TERM_HEADS), TERM_HEADS, returned):
        sums = add_terms(first, heads, width, parts, sums)

    outs = (mixed_out, grad_query, *sums)
    return lax.cond(
        any_seam > 0,
        lambda outs: any_lists(query_tok, key_tok, value_tok, out_weight, grad_out, tile_pairs),
        lambda outs: outs,
        outs,
    )


def solution(mesh):
    in_specs = (
        P("seq", "head"),
        P("seq", "head"),
        P("seq", "head"),
        P(None, "head"),
        P("seq", "head"),
        P("seq", None),
    )
    out_specs = (P("seq", "head"), P("seq", "head"), P("seq", "head"), P("seq", "head"))
    return jax.shard_map(
        on_device, mesh=mesh, in_specs=in_specs, out_specs=out_specs, check_vma=False
    )
```
